32 devices in a mesh: rows: 8 (over z, y), cols: 4 (over x, core).
Axes of the slice: x: 2, y: 2, z: 4, core: 2. Of those that a mesh axis runs over, the one named last changes fastest.
Arguments:
- snapshots: float32 [2048, 4096], P('rows', 'cols'), may hold values from -6 to 6
- flips: int32 [2048], P('rows'), may hold values 0 or 1
- sample_source: int32 [1024, 1], P('rows'), may hold values from 0 to 7; in each aligned block of 128 rows (0 to 127, 128 to 255, ...) at most 32 rows name the same one
- sample_offset: int32 [1024], P('rows'), may hold values from 0 to 255
- tile_index: int32 [16, 3], P('cols'), may hold values from 0 to 15
- tile_values: float32 [16, 3, 256, 256], P('cols'), may hold values from -0.21875 to 0.21875
Outputs:
- sketch: float32 [1024, 4096], P('rows', 'cols')
The draws below stay inside these ranges and needn't reach their ends.
Inputs may be any that keep to these rules, and one draw needn't show every extreme that they name: `sample_source`: among the 128 samples of one owner (one device's rows of this list) no source index appears more than 32 times, and in some owners' lists one appears exactly 32 times.
All inputs are finite; a program needn't handle non-finite values. No bound on the sum of `flips` on one device may be relied on, other than what follows from the above.
Results may differ from the reference program's by a relative error of at most 0.000088.
Values sent between devices are 32-bit elements; how exact they have to be, the bound alone decides.
A program may use at most 64 MiB of HBM per device.

```python
import math
import jax
import jax.numpy as jnp
import numpy as np
from jax import lax

C = 4096
TILE = 256
NNZ = 3
R_DEV = 256
S_DEV = 128
CAP = 32
TILES = 16
M = 2048
S_TOTAL = 1024
N_ROWS = 8


def place_ends(drawn, key, least, high):
    longest = drawn.shape.index(max(drawn.shape))
    spots = []
    for shift in (0, 1):
        where = [jax.random.randint(jax.random.fold_in(key, axis), (), 0, length) for axis, length in enumerate(drawn.shape)]
        where[longest] = (where[longest] + shift) % drawn.shape[longest]
        spots.append(tuple(where))
    return drawn.at[spots[0]].set(least).at[spots[1]].set(high)


def level_of(own_key, extent, shards, low, top_value):
    def one(axis_at, parts):
        heights = jax.random.uniform(jax.random.fold_in(jax.random.fold_in(own_key, 6), axis_at), (parts,), jnp.float32, low / len(shards), top_value / len(shards))
        return jnp.repeat(jnp.exp(heights), extent[axis_at] // parts).reshape((-1,) + (1,) * (len(extent) - axis_at - 1))

    loudness = one(*shards[0])
    for cut in shards[1:]:
        loudness = loudness * one(*cut)
    return loudness


def routed_block(key, own, number, rows, number_of, top, most, skew):
    order = jax.random.permutation(key, number_of)
    heavy_load, usual = load_shares(number_of, rows * top, most, skew, True), load_shares(number_of, rows * top, most, skew, False)
    places = jnp.arange(number_of)

    def named(tallies, offset_by):
        used = int((tallies > 0).sum())
        fixed = max(1, used // 4)
        passed = fixed + (places - fixed + offset_by * (used - fixed)) % max(1, number_of - fixed)
        return jnp.zeros((number_of,), jnp.int32).at[order[jnp.where(places < fixed, places, passed)]].set(jnp.asarray(tallies, jnp.int32))

    tallies = jnp.where(number % 4 == 0, named(heavy_load, number // 4), named(usual, number - number // 4 - 1))
    mixed = jax.random.permutation(jax.random.fold_in(own, 3), number_of)
    giver, receiver = mixed[0:number_of // 2 * 2:2], mixed[1:number_of // 2 * 2:2]
    slack = jnp.minimum(tallies[giver] - 1, most - tallies[receiver]) // 2
    slack = jnp.where((giver == order[0]) | (receiver == order[0]) | (tallies[receiver] == 0), 0, jnp.maximum(slack, 0))
    passed = jax.random.randint(jax.random.fold_in(own, 4), (number_of // 2,), 0, 1 << 20) % (slack + 1)
    tallies = tallies.at[giver].add(-passed).at[receiver].add(passed)
    items = jnp.searchsorted(jnp.cumsum(tallies), jnp.arange(rows * top), side="right").astype(jnp.int32)
    listing = items.reshape(top, rows).T
    listing = listing[jax.random.permutation(jax.random.fold_in(own, 1), rows)]
    offset_by = jax.random.randint(jax.random.fold_in(own, 2), (rows, 1), 0, top)
    return jnp.take_along_axis(listing, (jnp.arange(top)[None, :] + offset_by) % top, axis=1)


def load_shares(count, total, limit, slope, full):
    loads = [(1 << 20) // math.isqrt(rank ** slope) + 1 for rank in range(1, count + 1)]
    largest = limit if full else min(limit, max(-(-total // count), total * loads[0] // sum(loads)))
    least = 1 if total - largest >= count - 1 else 0
    holding, spare = [largest] + [least] * (count - 1), total - largest - least * (count - 1)
    while spare > 0:
        candidates = [i for i in range(1, count) if holding[i] < largest] or [i for i in range(1, count) if holding[i] < limit]
        mass, budget = sum([loads[i] for i in candidates]), spare
        for i in candidates:
            more = min(limit - holding[i], max(1, budget * loads[i] // mass), spare)
            holding[i] = holding[i] + more
            spare = spare - more
    return np.array(holding)


def centred(rng, extent, scale, most, cuts=(), kind=jnp.bfloat16):
    factor_of = level_of(rng, extent, cuts, -0.22, 0.18) if cuts else 1.0
    values = jax.random.normal(rng, extent, jnp.float32) * scale * factor_of
    return jnp.minimum(jnp.maximum(values, -most), most).astype(kind)


def setup_inputs(seed: int = 0) -> dict:
    key_list = jax.random.split(jax.random.key(seed), 7)
    snapshots = centred(key_list[0], (M, C), 1.0, 6.0, ((0, 8), (1, 4)), jnp.float32)
    flips = place_ends((jax.random.randint(key_list[1], (M,), 0, 2) < 1).astype(jnp.int32), jax.random.fold_in(key_list[1], 1), 0, 1)
    sample_source_keys = jax.random.split(jax.random.fold_in(key_list[2], 1), S_TOTAL // S_DEV)
    sample_source_turns = jax.random.permutation(jax.random.fold_in(key_list[2], 3), S_TOTAL // S_DEV)
    sample_source = jax.vmap(lambda own, number: routed_block(jax.random.fold_in(key_list[2], 2), own, number, S_DEV, N_ROWS, 1, CAP, 2))(sample_source_keys, sample_source_turns).reshape((S_TOTAL, 1))
    sample_offset = place_ends(jax.random.randint(key_list[3], (S_TOTAL,), 0, R_DEV), jax.random.fold_in(key_list[3], 1), 0, R_DEV - 1).astype(jnp.int32)
    tile_index = place_ends(jax.random.randint(key_list[4], (TILES, NNZ), 0, TILES), jax.random.fold_in(key_list[4], 1), 0, TILES - 1).astype(jnp.int32)
    tile_values = centred(key_list[5], (TILES, NNZ, TILE, TILE), (NNZ * TILE) ** -0.5, 0.21875, ((0, 4),), jnp.float32)
    return dict(snapshots=snapshots, flips=flips, sample_source=sample_source, sample_offset=sample_offset, tile_index=tile_index, tile_values=tile_values)


def walsh_hadamard(values):
    length = values.shape[0]
    columns = values.shape[1]
    stride = 1
    while stride < length:
        shaped = values.reshape(length // (2 * stride), 2, stride, columns)
        first = shaped[:, 0]
        second = shaped[:, 1]
        values = jnp.stack([first + second, first - second], axis=1).reshape(length, columns)
        stride = stride * 2
    return values

def apply_incidence(row_block, tile_index, tile_values):
    count = row_block.shape[0]
    pieces = row_block.reshape(count, TILES, TILE)

    def one_tile(pair):
        index_row, weights = pair
        chosen = jnp.take(pieces, index_row, axis=1)
        return jnp.einsum('nkc,kcd->nd', chosen, weights, precision=lax.Precision.HIGHEST)
    result = lax.map(one_tile, (tile_index, tile_values))
    return jnp.transpose(result, (1, 0, 2)).reshape(count, TILES * TILE)

def reference(snapshots, flips, sample_source, sample_offset, tile_index, tile_values):
    row_signs = (1 - 2 * flips).astype(jnp.float32)
    signed = snapshots * row_signs[:, None]
    transformed = walsh_hadamard(signed)
    row_ids = (sample_source[:, 0] * R_DEV + sample_offset).astype(jnp.int32)
    picked = jnp.take(transformed, row_ids, axis=0) * (1.0 / math.sqrt(S_TOTAL))
    return apply_incidence(picked, tile_index, tile_values)
```

```python
import functools
import math

import jax
import jax.numpy as jnp
from jax import lax
from jax.experimental import pallas as pl
from jax.experimental.pallas import tpu as pltpu
from jax.sharding import PartitionSpec as P

TILE = 256
LANES = 128
MESH = pl.DeviceIdType.MESH
HIGHEST = lax.Precision.HIGHEST


def swapped(array, axis, bit):
    return lax.ppermute(array, axis, [(i, i ^ 1 << bit) for i in range(lax.axis_size(axis))])


def parity_table(length):
    row_ids = lax.broadcasted_iota(jnp.int32, (length, length), 0)
    col_ids = lax.broadcasted_iota(jnp.int32, (length, length), 1)
    common = row_ids & col_ids
    parity = jnp.zeros((length, length), jnp.int32)
    for bit_level in range(length.bit_length()):
        parity = parity ^ common >> bit_level & 1
    return (1 - 2 * parity).astype(jnp.float32)


def incident(row_block, tile_index, tile_values):
    full_cols = lax.all_gather(row_block, "cols", axis=1, tiled=True)
    count = full_cols.shape[0]
    out = []
    for j in range(tile_index.shape[0]):
        total = jnp.zeros((count, TILE), jnp.float32)
        for k in range(tile_index.shape[1]):
            chosen = lax.dynamic_slice(full_cols, (0, tile_index[j, k] * TILE), (count, TILE))
            total = total + jnp.dot(chosen, tile_values[j, k], precision=HIGHEST)
        out.append(total)
    return jnp.concatenate(out, axis=1)


def general(snapshots, flips, sample_source, sample_offset, tile_index, tile_values):
    device_count = lax.axis_size("rows")
    local_rows = snapshots.shape[0]
    samples_here = sample_offset.shape[0]
    slot_cap = max(2, 2 * samples_here // device_count)
    row_signs = (1 - 2 * flips).astype(jnp.float32)
    signed = snapshots * row_signs[:, None]
    transformed = jnp.dot(parity_table(local_rows), signed, precision=HIGHEST)
    my_index = lax.axis_index("rows")
    for bit_level in range(device_count.bit_length() - 1):
        partner = swapped(transformed, "rows", bit_level)
        upper_half = my_index >> bit_level & 1 == 1
        transformed = jnp.where(upper_half, partner - transformed, transformed + partner)
    transformed = incident(transformed, tile_index, tile_values)
    own_source = sample_source[:, 0]
    all_source = lax.all_gather(own_source, "rows", axis=0, tiled=True)
    all_offset = lax.all_gather(sample_offset, "rows", axis=0, tiled=True)
    all_source = all_source.reshape(device_count, samples_here)
    all_offset = all_offset.reshape(device_count, samples_here)
    is_mine = all_source == my_index
    earlier_ids = lax.broadcasted_iota(jnp.int32, (samples_here, samples_here), 1)
    later_ids = lax.broadcasted_iota(jnp.int32, (samples_here, samples_here), 0)
    before = (later_ids < earlier_ids).astype(jnp.float32)
    slot_rank = jnp.dot(is_mine.astype(jnp.float32), before, precision=HIGHEST).astype(jnp.int32)
    slot_ids = lax.broadcasted_iota(jnp.int32, (1, 1, slot_cap), 2)
    slot_hit = is_mine[:, :, None] & (slot_rank[:, :, None] == slot_ids)
    slot_offset = jnp.sum(jnp.where(slot_hit, all_offset[:, :, None], 0), axis=1).reshape(-1)
    slot_used = jnp.any(slot_hit, axis=1).reshape(-1)
    local_ids = lax.broadcasted_iota(jnp.int32, (1, local_rows), 1)
    send_pick = ((slot_offset[:, None] == local_ids) & slot_used[:, None]).astype(jnp.float32)
    send_panel = jnp.dot(send_pick, transformed, precision=HIGHEST)
    received = lax.all_to_all(send_panel, "rows", split_axis=0, concat_axis=0, tiled=True)
    same_source = (own_source[None, :] == own_source[:, None]) & (earlier_ids < later_ids)
    own_rank = jnp.sum(same_source.astype(jnp.int32), axis=1)
    position = own_source * slot_cap + own_rank
    panel_ids = lax.broadcasted_iota(jnp.int32, (1, received.shape[0]), 1)
    own_pick = (position[:, None] == panel_ids).astype(jnp.float32)
    sketch_scale = 1.0 / math.sqrt(samples_here * device_count)
    return jnp.dot(own_pick, received, precision=HIGHEST) * sketch_scale


def flipped(index, mask):
    out, bit = index, 1
    while bit <= mask:
        if mask & bit:
            out = out + bit * (1 - 2 * ((index // bit) % 2))
        bit *= 2
    return out


def split(x):
    hi = x.astype(jnp.bfloat16)
    return hi, (x - hi.astype(jnp.float32)).astype(jnp.bfloat16)


def kernel(
    n, n_cols, scale,
    snap, meta, tile_index, tile_values, out,
    meta_all, recv, signs, total, picked, full, w, w_hi, w_lo,
    meta_s, meta_r, snap_s, snap_r, pick_s, pick_r, x_s, x_r, core_s, core_r, relay_s, relay_r, local_sem,
):
    rows = snap.shape[0]
    samples = total.shape[0] // n
    me, col = lax.axis_index("rows"), lax.axis_index("cols")
    across, beside = flipped(col, 2), flipped(col, 1)
    far_first = list(range(n - 1, 0, -1))
    near_first = list(range(1, n))

    def slot(c, r):
        return c * n + r

    load_own = pltpu.make_async_copy(
        snap.at[:, pl.ds(pl.multiple_of(me * LANES, LANES), LANES)], recv.at[me], local_sem.at[0]
    )
    load_w = pltpu.make_async_copy(tile_values, w, local_sem.at[1])
    load_meta = pltpu.make_async_copy(meta, meta_all.at[me], local_sem.at[2])
    load_own.start()
    load_w.start()
    load_meta.start()

    barrier = pltpu.get_barrier_semaphore()
    for mask in near_first:
        pl.semaphore_signal(barrier, inc=1, device_id={"rows": flipped(me, mask)}, device_id_type=MESH)
    for other in (across, beside):
        pl.semaphore_signal(barrier, inc=1, device_id={"cols": other}, device_id_type=MESH)
    pl.semaphore_wait(barrier, n + 1)

    def meta_copy(mask):
        return pltpu.make_async_remote_copy(
            src_ref=meta, dst_ref=meta_all.at[me], send_sem=meta_s.at[mask], recv_sem=meta_r.at[mask],
            device_id={"rows": flipped(me, mask)}, device_id_type=MESH,
        )

    def snap_copy(mask):
        other = flipped(me, mask)
        return pltpu.make_async_remote_copy(
            src_ref=snap.at[:, pl.ds(pl.multiple_of(other * LANES, LANES), LANES)],
            dst_ref=recv.at[me], send_sem=snap_s.at[mask], recv_sem=snap_r.at[mask],
            device_id={"rows": other}, device_id_type=MESH,
        )

    def pick_copy(mask):
        other = flipped(me, mask)
        return pltpu.make_async_remote_copy(
            src_ref=picked.at[other], dst_ref=full.at[slot(col, me)],
            send_sem=pick_s.at[mask], recv_sem=pick_r.at[mask],
            device_id={"rows": other}, device_id_type=MESH,
        )

    def col_copy(mask, owner, target, send, recv_sem):
        place = slot(owner, flipped(me, mask))
        return pltpu.make_async_remote_copy(
            src_ref=full.at[place], dst_ref=full.at[place],
            send_sem=send.at[mask], recv_sem=recv_sem.at[mask],
            device_id={"cols": target}, device_id_type=MESH,
        )

    x_copy = lambda mask: col_copy(mask, col, across, x_s, x_r)
    core_copy = lambda mask: col_copy(mask, col, beside, core_s, core_r)
    relay_copy = lambda mask: col_copy(mask, across, beside, relay_s, relay_r)

    for mask in far_first:
        meta_copy(mask).start()
    for mask in far_first:
        snap_copy(mask).start()

    load_w.wait()

    def split_w(i, carry):
        hi, lo = split(w[i])
        w_hi[i] = hi
        w_lo[i] = lo
        return carry

    lax.fori_loop(0, w.shape[0], split_w, 0)

    load_meta.wait()
    for mask in near_first:
        meta_copy(mask).wait_recv()
    lane = lax.broadcasted_iota(jnp.int32, (samples, LANES), 1)

    def owner_signs(d, carry):
        ids = jnp.broadcast_to(meta_all[d, 0:1, :], (samples, LANES)).T
        at = pl.ds(pl.multiple_of(d * samples, samples), samples)

        def block_signs(g, carry):
            for h in range(rows // LANES):
                common = ids & (lane + (g * rows + h * LANES))
                bits = 16
                while bits > 1:
                    bits //= 2
                    common = common ^ (common >> bits)
                parity = (common ^ meta_all[g, 1 + h : 2 + h, :]) & 1
                signs[g, at, h * LANES : (h + 1) * LANES] = (1 - 2 * parity).astype(jnp.float32).astype(jnp.bfloat16)
            return carry

        return lax.fori_loop(0, n, block_signs, carry)

    lax.fori_loop(0, n, owner_signs, 0)

    def halves(g):
        hi, lo = split(recv[g])
        return jnp.concatenate([hi, lo], axis=1)

    load_own.wait()
    for mask in range(n - 1):
        g = flipped(me, mask)
        if mask:
            snap_copy(mask).wait_recv()
        block = halves(g)

        def add_block(d, carry, g=g, block=block, first=mask == 0):
            at = pl.ds(pl.multiple_of(d * samples, samples), samples)
            part = jnp.dot(signs[g, at, :], block, preferred_element_type=jnp.float32)
            total[at, :] = part if first else total[at, :] + part
            return carry

        lax.fori_loop(0, n, add_block, 0)

    last = flipped(me, n - 1)
    snap_copy(n - 1).wait_recv()
    block = halves(last)
    for mask in far_first + [0]:
        d = flipped(me, mask)
        at = pl.ds(pl.multiple_of(d * samples, samples), samples)
        both = total[at, :] + jnp.dot(signs[last, at, :], block, preferred_element_type=jnp.float32)
        ready = (both[:, :LANES] + both[:, LANES:]) * scale
        if mask:
            picked[d] = ready
            pick_copy(mask).start()
        else:
            full[slot(col, me)] = ready

    for mask in range(n):
        if mask:
            pick_copy(mask).wait_recv()
        x_copy(mask).start()
        core_copy(mask).start()
    for mask in range(n):
        place = slot(across, flipped(me, mask))
        pltpu.make_async_remote_copy(
            src_ref=full.at[place], dst_ref=full.at[place], send_sem=x_s.at[mask], recv_sem=x_r.at[mask],
            device_id={"cols": across}, device_id_type=MESH,
        ).wait_recv()
        relay_copy(mask).start()
    for mask in range(n):
        core_copy(mask).wait_recv()
        relay_copy(mask).wait_recv()

    for j in range(tile_index.shape[0]):
        sums = jnp.zeros((samples, TILE), jnp.float32)
        for k in range(tile_index.shape[1]):
            t = tile_index[j, k]
            hi, lo = split(jnp.concatenate([full[2 * t], full[2 * t + 1]], axis=1))
            i = j * tile_index.shape[1] + k
            sums = sums + jnp.dot(hi, w_hi[i], preferred_element_type=jnp.float32)
            sums = sums + jnp.dot(lo, w_hi[i], preferred_element_type=jnp.float32)
            sums = sums + jnp.dot(hi, w_lo[i], preferred_element_type=jnp.float32)
        out[:, j * TILE : (j + 1) * TILE] = sums

    for mask in range(n):
        if mask:
            meta_copy(mask).wait_send()
            snap_copy(mask).wait_send()
            pick_copy(mask).wait_send()
        x_copy(mask).wait_send()
        core_copy(mask).wait_send()
        relay_copy(mask).wait_send()


def fused(snapshots, flips, sample_source, sample_offset, tile_index, tile_values):
    n, n_cols = lax.axis_size("rows"), lax.axis_size("cols")
    rows, width = snapshots.shape
    samples = sample_offset.shape[0]
    row_id = sample_source[:, 0] * rows + sample_offset
    meta = jnp.concatenate([row_id.reshape(1, LANES), flips.reshape(rows // LANES, LANES)], axis=0)
    meta = jnp.pad(meta, ((0, 8 - meta.shape[0]), (0, 0)))
    tiles, nnz = tile_index.shape
    weights = tile_values.reshape(tiles * nnz, TILE, TILE)
    scale = 1.0 / math.sqrt(samples * n)
    dma = pltpu.SemaphoreType.DMA((n,))
    return pl.pallas_call(
        functools.partial(kernel, n, n_cols, scale),
        out_shape=jax.ShapeDtypeStruct((samples, width), jnp.float32),
        in_specs=[
            pl.BlockSpec(memory_space=pl.ANY),
            pl.BlockSpec(memory_space=pltpu.VMEM),
            pl.BlockSpec(memory_space=pltpu.SMEM),
            pl.BlockSpec(memory_space=pl.ANY),
        ],
        out_specs=pl.BlockSpec(memory_space=pltpu.VMEM),
        scratch_shapes=[
            pltpu.VMEM((n, 8, LANES), jnp.int32),
            pltpu.VMEM((n, rows, LANES), jnp.float32),
            pltpu.VMEM((n, n * samples, rows), jnp.bfloat16),
            pltpu.VMEM((n * samples, 2 * LANES), jnp.float32),
            pltpu.VMEM((n, samples, LANES), jnp.float32),
            pltpu.VMEM((n_cols * n, samples, LANES), jnp.float32),
            pltpu.VMEM((tiles * nnz, TILE, TILE), jnp.float32),
            pltpu.VMEM((tiles * nnz, TILE, TILE), jnp.bfloat16),
            pltpu.VMEM((tiles * nnz, TILE, TILE), jnp.bfloat16),
        ]
        + [dma] * 12
        + [pltpu.SemaphoreType.DMA((3,))],
        compiler_params=pltpu.CompilerParams(
            collective_id=0, has_side_effects=True, vmem_limit_bytes=40 * 2**20
        ),
    )(snapshots, meta, tile_index, weights)


def on_device(snapshots, flips, sample_source, sample_offset, tile_index, tile_values):
    n, n_cols = lax.axis_size("rows"), lax.axis_size("cols")
    fits = (
        n & (n - 1) == 0
        and 2 <= n <= 8
        and n_cols == 4
        and snapshots.shape[1] == n * LANES
        and snapshots.shape[0] % LANES == 0
        and snapshots.shape[0] // LANES <= 7
        and sample_offset.shape[0] == LANES
    )
    return (fused if fits else general)(
        snapshots, flips, sample_source, sample_offset, tile_index, tile_values
    )


def solution(mesh):
    return jax.shard_map(
        on_device,
        mesh=mesh,
        in_specs=(
            P("rows", "cols"),
            P("rows"),
            P("rows", None),
            P("rows"),
            P("cols", None),
            P("cols", None, None, None),
        ),
        out_specs=P("rows", "cols"),
        check_vma=False,
    )
```

```python
import functools
import math

import jax
import jax.numpy as jnp
from jax import lax
from jax.experimental import pallas as pl
from jax.experimental.pallas import tpu as pltpu
from jax.sharding import PartitionSpec as P

TILE = 256
LANES = 128
MESH = pl.DeviceIdType.MESH
HIGHEST = lax.Precision.HIGHEST


def swapped(array, axis, bit):
    return lax.ppermute(array, axis, [(i, i ^ 1 << bit) for i in range(lax.axis_size(axis))])


def parity_table(length):
    row_ids = lax.broadcasted_iota(jnp.int32, (length, length), 0)
    col_ids = lax.broadcasted_iota(jnp.int32, (length, length), 1)
    common = row_ids & col_ids
    parity = jnp.zeros((length, length), jnp.int32)
    for bit_level in range(length.bit_length()):
        parity = parity ^ common >> bit_level & 1
    return (1 - 2 * parity).astype(jnp.float32)


def incident(row_block, tile_index, tile_values):
    full_cols = lax.all_gather(row_block, "cols", axis=1, tiled=True)
    count = full_cols.shape[0]
    out = []
    for j in range(tile_index.shape[0]):
        total = jnp.zeros((count, TILE), jnp.float32)
        for k in range(tile_index.shape[1]):
            chosen = lax.dynamic_slice(full_cols, (0, tile_index[j, k] * TILE), (count, TILE))
            total = total + jnp.dot(chosen, tile_values[j, k], precision=HIGHEST)
        out.append(total)
    return jnp.concatenate(out, axis=1)


def general(snapshots, flips, sample_source, sample_offset, tile_index, tile_values):
    device_count = lax.axis_size("rows")
    local_rows = snapshots.shape[0]
    samples_here = sample_offset.shape[0]
    slot_cap = max(2, 2 * samples_here // device_count)
    row_signs = (1 - 2 * flips).astype(jnp.float32)
    signed = snapshots * row_signs[:, None]
    transformed = jnp.dot(parity_table(local_rows), signed, precision=HIGHEST)
    my_index = lax.axis_index("rows")
    for bit_level in range(device_count.bit_length() - 1):
        partner = swapped(transformed, "rows", bit_level)
        upper_half = my_index >> bit_level & 1 == 1
        transformed = jnp.where(upper_half, partner - transformed, transformed + partner)
    transformed = incident(transformed, tile_index, tile_values)
    own_source = sample_source[:, 0]
    all_source = lax.all_gather(own_source, "rows", axis=0, tiled=True)
    all_offset = lax.all_gather(sample_offset, "rows", axis=0, tiled=True)
    all_source = all_source.reshape(device_count, samples_here)
    all_offset = all_offset.reshape(device_count, samples_here)
    is_mine = all_source == my_index
    earlier_ids = lax.broadcasted_iota(jnp.int32, (samples_here, samples_here), 1)
    later_ids = lax.broadcasted_iota(jnp.int32, (samples_here, samples_here), 0)
    before = (later_ids < earlier_ids).astype(jnp.float32)
    slot_rank = jnp.dot(is_mine.astype(jnp.float32), before, precision=HIGHEST).astype(jnp.int32)
    slot_ids = lax.broadcasted_iota(jnp.int32, (1, 1, slot_cap), 2)
    slot_hit = is_mine[:, :, None] & (slot_rank[:, :, None] == slot_ids)
    slot_offset = jnp.sum(jnp.where(slot_hit, all_offset[:, :, None], 0), axis=1).reshape(-1)
    slot_used = jnp.any(slot_hit, axis=1).reshape(-1)
    local_ids = lax.broadcasted_iota(jnp.int32, (1, local_rows), 1)
    send_pick = ((slot_offset[:, None] == local_ids) & slot_used[:, None]).astype(jnp.float32)
    send_panel = jnp.dot(send_pick, transformed, precision=HIGHEST)
    received = lax.all_to_all(send_panel, "rows", split_axis=0, concat_axis=0, tiled=True)
    same_source = (own_source[None, :] == own_source[:, None]) & (earlier_ids < later_ids)
    own_rank = jnp.sum(same_source.astype(jnp.int32), axis=1)
    position = own_source * slot_cap + own_rank
    panel_ids = lax.broadcasted_iota(jnp.int32, (1, received.shape[0]), 1)
    own_pick = (position[:, None] == panel_ids).astype(jnp.float32)
    sketch_scale = 1.0 / math.sqrt(samples_here * device_count)
    return jnp.dot(own_pick, received, precision=HIGHEST) * sketch_scale


def flipped(index, mask):
    out, bit = index, 1
    while bit <= mask:
        if mask & bit:
            out = out + bit * (1 - 2 * ((index // bit) % 2))
        bit *= 2
    return out


def split(x):
    hi = x.astype(jnp.bfloat16)
    return hi, (x - hi.astype(jnp.float32)).astype(jnp.bfloat16)


def kernel(
    n, scale,
    snap, flips, source, offset, tile_index, tile_values, out,
    meta, meta_all, own, recv, rhs, signs, sends, parts, full_a, full_b, w, w_cat,
    flips_v, source_v, offset_v, index_s,
    meta_s, meta_r, snap_s, snap_r, part_s, part_r, x_s, x_r, core_s, core_r, relay_s, relay_r, local_sem,
):
    group = n // 2
    rows = snap.shape[0]
    samples = parts.shape[2]
    tiles, nnz = tile_index.shape
    me, col = lax.axis_index("rows"), lax.axis_index("cols")
    place, first_row = me % group, me // group * group
    across, beside = flipped(col, 2), flipped(col, 1)

    local = [
        pltpu.make_async_copy(source, source_v, local_sem.at[0]),
        pltpu.make_async_copy(offset, offset_v, local_sem.at[1]),
        pltpu.make_async_copy(flips, flips_v, local_sem.at[2]),
        pltpu.make_async_copy(tile_index, index_s, local_sem.at[3]),
        pltpu.make_async_copy(
            snap.at[:, pl.ds(pl.multiple_of(place * TILE, TILE), TILE)], own, local_sem.at[4]
        ),
        pltpu.make_async_copy(tile_values, w, local_sem.at[5]),
    ]
    for copy in local:
        copy.start()

    barrier = pltpu.get_barrier_semaphore()
    for mask in range(1, n):
        pl.semaphore_signal(barrier, inc=1, device_id={"rows": flipped(me, mask)}, device_id_type=MESH)
    for other in (across, beside):
        pl.semaphore_signal(barrier, inc=1, device_id={"cols": other}, device_id_type=MESH)
    for copy in local[:3]:
        copy.wait()
    meta[...] = jnp.zeros_like(meta)
    meta[0:1, :] = source_v[...] * rows + offset_v[...]
    meta[1 : 1 + rows // LANES, :] = flips_v[...]
    meta_all[me] = meta[...]
    pl.semaphore_wait(barrier, n + 1)

    def meta_copy(mask):
        return pltpu.make_async_remote_copy(
            src_ref=meta, dst_ref=meta_all.at[me], send_sem=meta_s.at[mask], recv_sem=meta_r.at[mask],
            device_id={"rows": flipped(me, mask)}, device_id_type=MESH,
        )

    def snap_copy(q, mask):
        other = flipped(me, mask)
        start = pl.multiple_of((other % group) * TILE + q * LANES, LANES)
        return pltpu.make_async_remote_copy(
            src_ref=snap.at[:, pl.ds(start, LANES)], dst_ref=recv.at[q, place],
            send_sem=snap_s.at[q * group + mask], recv_sem=snap_r.at[q * group + mask],
            device_id={"rows": other}, device_id_type=MESH,
        )

    def part_copy(q, mask):
        return pltpu.make_async_remote_copy(
            src_ref=sends.at[q, mask], dst_ref=parts.at[q, me],
            send_sem=part_s.at[q * n + mask], recv_sem=part_r.at[q * n + mask],
            device_id={"rows": flipped(me, mask)}, device_id_type=MESH,
        )

    full = (full_a, full_b)

    def slot(c, mask):
        return c * group + flipped(me, mask) % group

    def col_copy(owner, q, mask, target, send, receive):
        at = slot(owner, mask)
        return pltpu.make_async_remote_copy(
            src_ref=full[q].at[at], dst_ref=full[q].at[at],
            send_sem=send.at[q * group + mask], recv_sem=receive.at[q * group + mask],
            device_id={"cols": target}, device_id_type=MESH,
        )

    x_copy = lambda q, mask: col_copy(col, q, mask, across, x_s, x_r)
    core_copy = lambda q, mask: col_copy(col, q, mask, beside, core_s, core_r)
    relay_copy = lambda q, mask: col_copy(across, q, mask, beside, relay_s, relay_r)

    for mask in range(n - 1, 0, -1):
        meta_copy(mask).start()
    for q in range(2):
        for mask in range(group - 1, 0, -1):
            snap_copy(q, mask).start()

    for mask in range(1, n):
        meta_copy(mask).wait_recv()
    lane = lax.broadcasted_iota(jnp.int32, (samples, LANES), 1)

    def folded(bits, width):
        while width > 1:
            width //= 2
            bits = bits ^ (bits >> width)
        return bits

    def owner_signs(d, carry):
        ids = jnp.broadcast_to(meta_all[d, 0:1, :], (samples, LANES)).T
        at = pl.ds(pl.multiple_of(d * samples, samples), samples)
        inner = [folded(ids & (lane + h * LANES), 16) for h in range(rows // LANES)]
        for g in range(group):
            outer = folded(ids & ((first_row + g) * rows), 16)
            for h in range(rows // LANES):
                parity = (inner[h] ^ outer ^ meta_all[first_row + g, 1 + h : 2 + h, :]) & 1
                begin = g * rows + h * LANES
                signs[at, begin : begin + LANES] = jnp.where(parity == 0, 1.0, -1.0).astype(jnp.bfloat16)
        return carry

    lax.fori_loop(0, n, owner_signs, 0)

    def put_rhs(q, g, block):
        hi, lo = split(block)
        at = pl.ds(pl.multiple_of(g * rows, rows), rows)
        rhs[q, at, 0:LANES] = hi
        rhs[q, at, LANES : 2 * LANES] = lo

    local[4].wait()
    for q in range(2):
        put_rhs(q, place, own[:, q * LANES : (q + 1) * LANES])

    def send_parts(q):
        for mask in range(1, group):
            snap_copy(q, mask).wait_recv()
            g = flipped(me, mask) % group
            put_rhs(q, g, recv[q, g])
        for mask in range(n - 1, -1, -1):
            d = flipped(me, mask)
            at = pl.ds(pl.multiple_of(d * samples, samples), samples)
            both = jnp.dot(signs[at, :], rhs[q], preferred_element_type=jnp.float32)
            ready = (both[:, :LANES] + both[:, LANES:]) * scale
            if mask:
                sends[q, mask] = ready
                part_copy(q, mask).start()
            else:
                parts[q, me] = ready

    send_parts(0)

    local[5].wait()

    def split_w(j, carry):
        for k in range(nnz):
            for q in range(2):
                hi, lo = split(w[j * nnz + k, q * LANES : (q + 1) * LANES, :])
                begin = 3 * k * LANES
                w_cat[q, j, begin : begin + LANES, :] = hi
                w_cat[q, j, begin + LANES : begin + 2 * LANES, :] = hi
                w_cat[q, j, begin + 2 * LANES : begin + 3 * LANES, :] = lo
        return carry

    lax.fori_loop(0, tiles, split_w, 0)

    send_parts(1)
    local[3].wait()

    for q in range(2):
        for mask in range(group):
            if mask:
                part_copy(q, mask).wait_recv()
            part_copy(q, mask + group).wait_recv()
            near, far = flipped(me, mask), flipped(me, mask + group)
            full[q][slot(col, mask)] = parts[q, near] + parts[q, far]
            x_copy(q, mask).start()
            core_copy(q, mask).start()
        for mask in range(group):
            col_copy(across, q, mask, across, x_s, x_r).wait_recv()
            relay_copy(q, mask).start()
        for mask in range(group):
            core_copy(q, mask).wait_recv()
            relay_copy(q, mask).wait_recv()
        for j in range(tiles):
            pieces = []
            for k in range(nnz):
                hi, lo = split(full[q][index_s[j, k]])
                pieces += [hi, lo, hi]
            sums = jnp.dot(jnp.concatenate(pieces, axis=1), w_cat[q, j], preferred_element_type=jnp.float32)
            at = slice(j * TILE, (j + 1) * TILE)
            out[:, at] = out[:, at] + sums if q else sums

    for mask in range(1, n):
        meta_copy(mask).wait_send()
    for q in range(2):
        for mask in range(1, n):
            part_copy(q, mask).wait_send()
        for mask in range(group):
            if mask:
                snap_copy(q, mask).wait_send()
            x_copy(q, mask).wait_send()
            core_copy(q, mask).wait_send()
            relay_copy(q, mask).wait_send()


def fused(snapshots, flips, sample_source, sample_offset, tile_index, tile_values):
    n, n_cols = lax.axis_size("rows"), lax.axis_size("cols")
    group = n // 2
    rows, width = snapshots.shape
    samples = sample_offset.shape[0]
    tiles, nnz = tile_index.shape
    weights = tile_values.reshape(tiles * nnz, TILE, TILE)
    scale = 1.0 / math.sqrt(samples * n)
    dma = lambda count: [pltpu.SemaphoreType.DMA((count,))] * 2
    return pl.pallas_call(
        functools.partial(kernel, n, scale),
        out_shape=jax.ShapeDtypeStruct((samples, width), jnp.float32),
        in_specs=[pl.BlockSpec(memory_space=pl.ANY)] * 6,
        out_specs=pl.BlockSpec(memory_space=pltpu.VMEM),
        scratch_shapes=[
            pltpu.VMEM((8, LANES), jnp.int32),
            pltpu.VMEM((n, 8, LANES), jnp.int32),
            pltpu.VMEM((rows, TILE), jnp.float32),
            pltpu.VMEM((2, group, rows, LANES), jnp.float32),
            pltpu.VMEM((2, group * rows, 2 * LANES), jnp.bfloat16),
            pltpu.VMEM((n * samples, group * rows), jnp.bfloat16),
            pltpu.VMEM((2, n, samples, LANES), jnp.float32),
            pltpu.VMEM((2, n, samples, LANES), jnp.float32),
            pltpu.VMEM((n_cols * group, samples, LANES), jnp.float32),
            pltpu.VMEM((n_cols * group, samples, LANES), jnp.float32),
            pltpu.VMEM((tiles * nnz, TILE, TILE), jnp.float32),
            pltpu.VMEM((2, tiles, 3 * nnz * LANES, TILE), jnp.bfloat16),
            pltpu.VMEM((rows // LANES, LANES), jnp.int32),
            pltpu.VMEM((1, LANES), jnp.int32),
            pltpu.VMEM((1, LANES), jnp.int32),
            pltpu.SMEM((tiles, nnz), jnp.int32),
        ]
        + dma(n) + dma(2 * group) + dma(2 * n) + dma(2 * group) + dma(2 * group) + dma(2 * group)
        + [pltpu.SemaphoreType.DMA((6,))],
        compiler_params=pltpu.CompilerParams(
            collective_id=0, has_side_effects=True, vmem_limit_bytes=60 * 2**20
        ),
    )(
        snapshots, flips.reshape(rows // LANES, LANES), sample_source.reshape(1, samples),
        sample_offset.reshape(1, samples), tile_index, weights,
    )


def on_device(snapshots, flips, sample_source, sample_offset, tile_index, tile_values):
    n, n_cols = lax.axis_size("rows"), lax.axis_size("cols")
    rows = snapshots.shape[0]
    fits = (
        n & (n - 1) == 0
        and 2 <= n <= 8
        and n_cols == 4
        and snapshots.shape[1] == n // 2 * TILE
        and rows & (rows - 1) == 0
        and LANES <= rows <= 4 * LANES
        and sample_offset.shape[0] == LANES
    )
    return (fused if fits else general)(
        snapshots, flips, sample_source, sample_offset, tile_index, tile_values
    )


def solution(mesh):
    return jax.shard_map(
        on_device,
        mesh=mesh,
        in_specs=(
            P("rows", "cols"),
            P("rows"),
            P("rows", None),
            P("rows"),
            P("cols", None),
            P("cols", None, None, None),
        ),
        out_specs=P("rows", "cols"),
        check_vma=False,
    )
```

```python
import functools
import math

import jax
import jax.numpy as jnp
from jax import lax
from jax.experimental import pallas as pl
from jax.experimental.pallas import tpu as pltpu
from jax.sharding import PartitionSpec as P

TILE = 256
LANES = 128
MESH = pl.DeviceIdType.MESH
HIGHEST = lax.Precision.HIGHEST
WINDOW = 5


def swapped(array, axis, bit):
    return lax.ppermute(array, axis, [(i, i ^ 1 << bit) for i in range(lax.axis_size(axis))])


def parity_table(length):
    row_ids = lax.broadcasted_iota(jnp.int32, (length, length), 0)
    col_ids = lax.broadcasted_iota(jnp.int32, (length, length), 1)
    common = row_ids & col_ids
    parity = jnp.zeros((length, length), jnp.int32)
    for bit_level in range(length.bit_length()):
        parity = parity ^ common >> bit_level & 1
    return (1 - 2 * parity).astype(jnp.float32)


def incident(row_block, tile_index, tile_values):
    full_cols = lax.all_gather(row_block, "cols", axis=1, tiled=True)
    count = full_cols.shape[0]
    out = []
    for j in range(tile_index.shape[0]):
        total = jnp.zeros((count, TILE), jnp.float32)
        for k in range(tile_index.shape[1]):
            chosen = lax.dynamic_slice(full_cols, (0, tile_index[j, k] * TILE), (count, TILE))
            total = total + jnp.dot(chosen, tile_values[j, k], precision=HIGHEST)
        out.append(total)
    return jnp.concatenate(out, axis=1)


def general(snapshots, flips, sample_source, sample_offset, tile_index, tile_values):
    device_count = lax.axis_size("rows")
    local_rows = snapshots.shape[0]
    samples_here = sample_offset.shape[0]
    slot_cap = max(2, 2 * samples_here // device_count)
    row_signs = (1 - 2 * flips).astype(jnp.float32)
    signed = snapshots * row_signs[:, None]
    transformed = jnp.dot(parity_table(local_rows), signed, precision=HIGHEST)
    my_index = lax.axis_index("rows")
    for bit_level in range(device_count.bit_length() - 1):
        partner = swapped(transformed, "rows", bit_level)
        upper_half = my_index >> bit_level & 1 == 1
        transformed = jnp.where(upper_half, partner - transformed, transformed + partner)
    transformed = incident(transformed, tile_index, tile_values)
    own_source = sample_source[:, 0]
    all_source = lax.all_gather(own_source, "rows", axis=0, tiled=True)
    all_offset = lax.all_gather(sample_offset, "rows", axis=0, tiled=True)
    all_source = all_source.reshape(device_count, samples_here)
    all_offset = all_offset.reshape(device_count, samples_here)
    is_mine = all_source == my_index
    earlier_ids = lax.broadcasted_iota(jnp.int32, (samples_here, samples_here), 1)
    later_ids = lax.broadcasted_iota(jnp.int32, (samples_here, samples_here), 0)
    before = (later_ids < earlier_ids).astype(jnp.float32)
    slot_rank = jnp.dot(is_mine.astype(jnp.float32), before, precision=HIGHEST).astype(jnp.int32)
    slot_ids = lax.broadcasted_iota(jnp.int32, (1, 1, slot_cap), 2)
    slot_hit = is_mine[:, :, None] & (slot_rank[:, :, None] == slot_ids)
    slot_offset = jnp.sum(jnp.where(slot_hit, all_offset[:, :, None], 0), axis=1).reshape(-1)
    slot_used = jnp.any(slot_hit, axis=1).reshape(-1)
    local_ids = lax.broadcasted_iota(jnp.int32, (1, local_rows), 1)
    send_pick = ((slot_offset[:, None] == local_ids) & slot_used[:, None]).astype(jnp.float32)
    send_panel = jnp.dot(send_pick, transformed, precision=HIGHEST)
    received = lax.all_to_all(send_panel, "rows", split_axis=0, concat_axis=0, tiled=True)
    same_source = (own_source[None, :] == own_source[:, None]) & (earlier_ids < later_ids)
    own_rank = jnp.sum(same_source.astype(jnp.int32), axis=1)
    position = own_source * slot_cap + own_rank
    panel_ids = lax.broadcasted_iota(jnp.int32, (1, received.shape[0]), 1)
    own_pick = (position[:, None] == panel_ids).astype(jnp.float32)
    sketch_scale = 1.0 / math.sqrt(samples_here * device_count)
    return jnp.dot(own_pick, received, precision=HIGHEST) * sketch_scale


def flipped(index, mask):
    out, bit = index, 1
    while bit <= mask:
        if mask & bit:
            out = out + bit * (1 - 2 * ((index // bit) % 2))
        bit *= 2
    return out


def split(x):
    hi = x.astype(jnp.bfloat16)
    return hi, (x - hi.astype(jnp.float32)).astype(jnp.bfloat16)


def kernel(
    n, scale,
    snap, flips, source, offset, tile_index, tile_values, out,
    meta, meta_all, own, recv, rhs, signs, sends, parts, full_a, full_b, w, w_cat,
    flips_v, source_v, offset_v, index_s,
    meta_s, meta_r, snap_s, snap_r, part_s, part_r, x_s, x_r, core_s, core_r, relay_s, relay_r, local_sem,
):
    group = n // 2
    rows = snap.shape[0]
    samples = parts.shape[2]
    tiles, nnz = tile_index.shape
    me, col = lax.axis_index("rows"), lax.axis_index("cols")
    place, first_row = me % group, me // group * group
    across, beside = flipped(col, 2), flipped(col, 1)

    local = [
        pltpu.make_async_copy(source, source_v, local_sem.at[0]),
        pltpu.make_async_copy(offset, offset_v, local_sem.at[1]),
        pltpu.make_async_copy(flips, flips_v, local_sem.at[2]),
        pltpu.make_async_copy(tile_index, index_s, local_sem.at[3]),
        pltpu.make_async_copy(
            snap.at[:, pl.ds(pl.multiple_of(place * TILE, TILE), TILE)], own, local_sem.at[4]
        ),
        pltpu.make_async_copy(tile_values, w, local_sem.at[5]),
    ]
    for copy in local:
        copy.start()

    barrier = pltpu.get_barrier_semaphore()
    for mask in range(1, n):
        pl.semaphore_signal(barrier, inc=1, device_id={"rows": flipped(me, mask)}, device_id_type=MESH)
    for other in (across, beside):
        pl.semaphore_signal(barrier, inc=1, device_id={"cols": other}, device_id_type=MESH)
    for copy in local[:3]:
        copy.wait()
    meta[...] = jnp.zeros_like(meta)
    meta[0:1, :] = source_v[...] * rows + offset_v[...]
    meta[1 : 1 + rows // LANES, :] = flips_v[...]
    meta_all[me] = meta[...]
    pl.semaphore_wait(barrier, n + 1)

    def meta_copy(mask):
        return pltpu.make_async_remote_copy(
            src_ref=meta, dst_ref=meta_all.at[me], send_sem=meta_s.at[mask], recv_sem=meta_r.at[mask],
            device_id={"rows": flipped(me, mask)}, device_id_type=MESH,
        )

    def snap_copy(q, mask):
        other = flipped(me, mask)
        start = pl.multiple_of((other % group) * TILE + q * LANES, LANES)
        return pltpu.make_async_remote_copy(
            src_ref=snap.at[:, pl.ds(start, LANES)], dst_ref=recv.at[q, place],
            send_sem=snap_s.at[q * group + mask], recv_sem=snap_r.at[q * group + mask],
            device_id={"rows": other}, device_id_type=MESH,
        )

    def part_copy(q, mask):
        return pltpu.make_async_remote_copy(
            src_ref=sends.at[q, mask], dst_ref=parts.at[q, me],
            send_sem=part_s.at[q * n + mask], recv_sem=part_r.at[q * n + mask],
            device_id={"rows": flipped(me, mask)}, device_id_type=MESH,
        )

    full = (full_a, full_b)

    def slot(c, mask):
        return c * group + flipped(me, mask) % group

    def col_copy(owner, q, mask, target, send, receive):
        at = slot(owner, mask)
        return pltpu.make_async_remote_copy(
            src_ref=full[q].at[at], dst_ref=full[q].at[at],
            send_sem=send.at[q * group + mask], recv_sem=receive.at[q * group + mask],
            device_id={"cols": target}, device_id_type=MESH,
        )

    x_copy = lambda q, mask: col_copy(col, q, mask, across, x_s, x_r)
    core_copy = lambda q, mask: col_copy(col, q, mask, beside, core_s, core_r)
    relay_copy = lambda q, mask: col_copy(across, q, mask, beside, relay_s, relay_r)

    for mask in range(n - 1, 0, -1):
        meta_copy(mask).start()
    for mask in range(group - 1, 0, -1):
        snap_copy(0, mask).start()

    for mask in range(1, n):
        meta_copy(mask).wait_recv()
    lane = lax.broadcasted_iota(jnp.int32, (samples, LANES), 1)

    def folded(bits, width):
        while width > 1:
            width //= 2
            bits = bits ^ (bits >> width)
        return bits

    def owner_signs(d, carry):
        ids = jnp.broadcast_to(meta_all[d, 0:1, :], (samples, LANES)).T
        at = pl.ds(pl.multiple_of(d * samples, samples), samples)
        inner = [folded(ids & (lane + h * LANES), 16) for h in range(rows // LANES)]
        for g in range(group):
            outer = folded(ids & ((first_row + g) * rows), 16)
            for h in range(rows // LANES):
                parity = (inner[h] ^ outer ^ meta_all[first_row + g, 1 + h : 2 + h, :]) & 1
                begin = g * rows + h * LANES
                signs[at, begin : begin + LANES] = jnp.where(parity == 0, 1.0, -1.0).astype(jnp.bfloat16)
        return carry

    lax.fori_loop(0, n, owner_signs, 0)

    def put_rhs(q, g, block):
        hi, lo = split(block)
        at = pl.ds(pl.multiple_of(g * rows, rows), rows)
        rhs[q, at, 0:LANES] = hi
        rhs[q, at, LANES : 2 * LANES] = lo

    local[4].wait()
    for q in range(2):
        put_rhs(q, place, own[:, q * LANES : (q + 1) * LANES])

    def arrive(q):
        for mask in range(1, group):
            snap_copy(q, mask).wait_recv()
            g = flipped(me, mask) % group
            put_rhs(q, g, recv[q, g])

    def part(q, mask):
        at = pl.ds(pl.multiple_of(flipped(me, mask) * samples, samples), samples)
        both = jnp.dot(signs[at, :], rhs[q], preferred_element_type=jnp.float32)
        return (both[:, :LANES] + both[:, LANES:]) * scale

    order = [group] + [m for i in range(1, group) for m in (i, group + i)]
    queue = [(q, mask) for q in range(2) for mask in order]

    def send_part(at):
        q, mask = queue[at]
        sends[q, mask] = part(q, mask)
        if at >= WINDOW:
            part_copy(*queue[at - WINDOW]).wait_send()
        part_copy(q, mask).start()

    def piece(q, mask):
        if mask:
            part_copy(q, mask).wait_recv()
        part_copy(q, mask + group).wait_recv()
        full[q][slot(col, mask)] = parts[q, flipped(me, mask)] + parts[q, flipped(me, mask + group)]
        x_copy(q, mask).start()
        core_copy(q, mask).start()

    def relay(q, mask):
        col_copy(across, q, mask, across, x_s, x_r).wait_recv()
        relay_copy(q, mask).start()

    arrive(0)
    for mask in range(group - 1, 0, -1):
        snap_copy(1, mask).start()
    for at in range(WINDOW):
        send_part(at)
    parts[0, me] = part(0, 0)

    local[5].wait()

    def split_w(j, carry):
        for k in range(nnz):
            for q in range(2):
                hi, lo = split(w[j * nnz + k, q * LANES : (q + 1) * LANES, :])
                begin = 3 * k * LANES
                w_cat[q, j, begin : begin + LANES, :] = hi
                w_cat[q, j, begin + LANES : begin + 2 * LANES, :] = hi
                w_cat[q, j, begin + 2 * LANES : begin + 3 * LANES, :] = lo
        return carry

    lax.fori_loop(0, tiles, split_w, 0)

    for at in range(WINDOW, len(order)):
        send_part(at)
    local[3].wait()
    arrive(1)
    todo = [(piece, mask) for mask in range(group)] + [(relay, mask) for mask in range(group)]
    for at in range(len(order)):
        send_part(len(order) + at)
        if at == 0:
            parts[1, me] = part(1, 0)
        else:
            step, mask = todo.pop(0)
            step(0, mask)
    for step, mask in todo:
        step(0, mask)

    def incidence(q):
        for mask in range(group):
            core_copy(q, mask).wait_recv()
            relay_copy(q, mask).wait_recv()
        for j in range(tiles):
            pieces = []
            for k in range(nnz):
                hi, lo = split(full[q][index_s[j, k]])
                pieces += [hi, lo, hi]
            sums = jnp.dot(jnp.concatenate(pieces, axis=1), w_cat[q, j], preferred_element_type=jnp.float32)
            at = slice(j * TILE, (j + 1) * TILE)
            out[:, at] = out[:, at] + sums if q else sums

    incidence(0)
    for mask in range(group):
        piece(1, mask)
        if mask:
            relay(1, mask - 1)
    relay(1, group - 1)
    incidence(1)

    for mask in range(1, n):
        meta_copy(mask).wait_send()
    for copy in queue[-WINDOW:]:
        part_copy(*copy).wait_send()
    for q in range(2):
        for mask in range(group):
            if mask:
                snap_copy(q, mask).wait_send()
            x_copy(q, mask).wait_send()
            core_copy(q, mask).wait_send()
            relay_copy(q, mask).wait_send()


def fused(snapshots, flips, sample_source, sample_offset, tile_index, tile_values):
    n, n_cols = lax.axis_size("rows"), lax.axis_size("cols")
    group = n // 2
    rows, width = snapshots.shape
    samples = sample_offset.shape[0]
    tiles, nnz = tile_index.shape
    weights = tile_values.reshape(tiles * nnz, TILE, TILE)
    scale = 1.0 / math.sqrt(samples * n)
    dma = lambda count: [pltpu.SemaphoreType.DMA((count,))] * 2
    return pl.pallas_call(
        functools.partial(kernel, n, scale),
        out_shape=jax.ShapeDtypeStruct((samples, width), jnp.float32),
        in_specs=[pl.BlockSpec(memory_space=pl.ANY)] * 6,
        out_specs=pl.BlockSpec(memory_space=pltpu.VMEM),
        scratch_shapes=[
            pltpu.VMEM((8, LANES), jnp.int32),
            pltpu.VMEM((n, 8, LANES), jnp.int32),
            pltpu.VMEM((rows, TILE), jnp.float32),
            pltpu.VMEM((2, group, rows, LANES), jnp.float32),
            pltpu.VMEM((2, group * rows, 2 * LANES), jnp.bfloat16),
            pltpu.VMEM((n * samples, group * rows), jnp.bfloat16),
            pltpu.VMEM((2, n, samples, LANES), jnp.float32),
            pltpu.VMEM((2, n, samples, LANES), jnp.float32),
            pltpu.VMEM((n_cols * group, samples, LANES), jnp.float32),
            pltpu.VMEM((n_cols * group, samples, LANES), jnp.float32),
            pltpu.VMEM((tiles * nnz, TILE, TILE), jnp.float32),
            pltpu.VMEM((2, tiles, 3 * nnz * LANES, TILE), jnp.bfloat16),
            pltpu.VMEM((rows // LANES, LANES), jnp.int32),
            pltpu.VMEM((1, LANES), jnp.int32),
            pltpu.VMEM((1, LANES), jnp.int32),
            pltpu.SMEM((tiles, nnz), jnp.int32),
        ]
        + dma(n) + dma(2 * group) + dma(2 * n) + dma(2 * group) + dma(2 * group) + dma(2 * group)
        + [pltpu.SemaphoreType.DMA((6,))],
        compiler_params=pltpu.CompilerParams(
            collective_id=0, has_side_effects=True, vmem_limit_bytes=60 * 2**20
        ),
    )(
        snapshots, flips.reshape(rows // LANES, LANES), sample_source.reshape(1, samples),
        sample_offset.reshape(1, samples), tile_index, weights,
    )


def on_device(snapshots, flips, sample_source, sample_offset, tile_index, tile_values):
    n, n_cols = lax.axis_size("rows"), lax.axis_size("cols")
    rows = snapshots.shape[0]
    fits = (
        n & (n - 1) == 0
        and 2 <= n <= 8
        and n_cols == 4
        and snapshots.shape[1] == n // 2 * TILE
        and rows & (rows - 1) == 0
        and LANES <= rows <= 4 * LANES
        and sample_offset.shape[0] == LANES
    )
    return (fused if fits else general)(
        snapshots, flips, sample_source, sample_offset, tile_index, tile_values
    )


def solution(mesh):
    return jax.shard_map(
        on_device,
        mesh=mesh,
        in_specs=(
            P("rows", "cols"),
            P("rows"),
            P("rows", None),
            P("rows"),
            P("cols", None),
            P("cols", None, None, None),
        ),
        out_specs=P("rows", "cols"),
        check_vma=False,
    )
```
